32 devices in a mesh: parts: 2 (over y), tile: 4 (over z), slide: 4 (over x, core), chan: 1.
Axes of the slice: x: 2, y: 2, z: 4, core: 2. Of those that a mesh axis runs over, the one named last changes fastest.
Arguments:
- residual_pool: bfloat16 [16, 20, 7, 7, 2048], P(('parts', 'slide'), 'tile', None, None, 'chan'), parts along dimension 0, may hold values from -8 to 8
- inner_pool: bfloat16 [16, 20, 7, 7, 2048], P(('parts', 'slide'), 'tile', None, None, 'chan'), parts along dimension 0, may hold values from -6 to 6
- window_index: int32 [16, 16], P(('parts', 'slide'), 'tile'), parts along dimension 0, may hold values from 0 to 4, as said below
- labels: int32 [16], P(('parts', 'slide')), parts along dimension 0, may hold values from 0 to 3
- group_weight: bfloat16 [3, 3, 64, 2048], P(None, None, None, 'chan'), may hold values from -2 to 2
- expand_weight: bfloat16 [2048, 2048], P(None, 'chan'), may hold values from -0.125 to 0.125
- attn_proj: bfloat16 [2, 2048, 256], P(None, 'chan'), may hold values from -0.5 to 0.5
- attn_vector: bfloat16 [256, 8], replicated, may hold values from -0.29882812 to 0.29882812
- classifier: bfloat16 [8, 2048, 4], P(None, 'chan'), may hold values from -0.046875 to 0.046875
Outputs:
- slide_loss: float32 [16], P(('parts', 'slide')), parts along dimension 0
- dir_w2: bfloat16 [6, 3, 64, 2048], P('parts', None, None, 'chan'), parts along dimension 0
- dir_w3: float32 [4096, 2048], P(('parts', 'tile', 'slide'), 'chan'), parts along dimension 0
- dir_proj: bfloat16 [4, 2048, 256], P('parts', 'chan'), parts along dimension 0
- dir_vector: float32 [512, 8], P('parts'), parts along dimension 0
- dir_class: float32 [16, 2048, 4], P('parts', 'chan'), parts along dimension 0
The draws below stay inside these ranges and needn't reach their ends.
There are 2 independent parts, one for each index of `parts`. The reference program is written for one: setup_inputs(seed, part) draws one part's arguments, and reference() takes and returns one part's arrays. A program takes and returns all parts, laid end to end along the dimension named above; an argument that names none is the same for every part. Nothing has to cross between parts.
Inputs may be any that keep to these rules, and one draw needn't show every extreme that they name: `window_index`: within each aligned block of 4 window positions of a slide the entries are distinct indices into that block's 5 stored tiles.
All inputs are finite; a program needn't handle non-finite values.
Results may differ from the reference program's by a relative error of at most 0.013.
The reference program's roundings to bfloat16 on the way count: a program that leaves them out, or rounds other values in their place, can miss the bound.
Values may be sent and summed in bfloat16 or wider, within the bound.
A program may use at most 128 MiB of HBM per device.

```python
import jax
import jax.numpy as jnp
from jax import lax

C = 2048
GROUPS = 32
GW = 64
HW = 7
ATT = 256
HEADS = 8
NCLS = 4
TILE_DEV = 4
POOL_DEV = 5
WINDOW = 16
POOL = 20
SLIDES = 8


def draw_residual_pool(key, part):
    key_mean, key_noise = jax.random.split(key, 2)
    shape_all = (SLIDES, POOL, HW, HW, C)
    tile_mean = 1.5 * jax.random.normal(key_mean, (SLIDES, POOL, 1, 1, C), jnp.float32)
    noise_part = 0.7 * jax.random.normal(key_noise, shape_all, jnp.float32)
    values = tile_mean + noise_part
    return jnp.clip(values, -8.0, 8.0).astype(jnp.bfloat16)


def draw_group_weight(key, part):
    key_base, key_scale = jax.random.split(key, 2)
    rising = jnp.exp(jnp.log(3.0) * jnp.arange(C, dtype=jnp.float32) / C)
    base = jnp.clip(jax.random.normal(key_base, (3, 3, GW, C), jnp.float32), -4.0, 4.0)
    spread = jnp.exp(jax.random.uniform(key_scale, (C,), jnp.float32, 0.0, 2.3))
    values = base * (rising * spread * 0.25) / jnp.sqrt(9.0 * GW)
    return jnp.clip(values, -2.0, 2.0).astype(jnp.bfloat16)


def draw_window_index(key, part):
    blocks = SLIDES * (WINDOW // TILE_DEV)
    ranking = jax.random.randint(key, (blocks, POOL_DEV), 0, 1 << 20) * POOL_DEV + jnp.arange(POOL_DEV, dtype=jnp.int32)[None, :]
    ordering = jnp.argsort(ranking, axis=1)
    return ordering[:, :TILE_DEV].reshape(SLIDES, WINDOW).astype(jnp.int32)


def set_ends(array, rng, smallest, top_value):
    longest = array.shape.index(max(array.shape))
    spots = []
    for shift in (0, 1):
        where = [jax.random.randint(jax.random.fold_in(rng, axis), (), 0, length) for axis, length in enumerate(array.shape)]
        where[longest] = (where[longest] + shift) % array.shape[longest]
        spots.append(tuple(where))
    return array.at[spots[0]].set(smallest).at[spots[1]].set(top_value)


def levels(own_key, extent, pieces, smallest, high):
    gain = 1.0
    for dim, blocks in pieces:
        heights = jax.random.uniform(jax.random.fold_in(jax.random.fold_in(own_key, 6), dim), (blocks,), jnp.float32, smallest / len(pieces), high / len(pieces))
        gain = gain * jnp.repeat(jnp.exp(heights), extent[dim] // blocks).reshape((-1,) + (1,) * (len(extent) - 1 - dim))
    return gain


def normal_values(own_key, extent, scale, limit, cuts=(), kind=jnp.bfloat16):
    array = jax.random.normal(own_key, extent, jnp.float32) * scale
    if len(cuts) > 0:
        array = levels(own_key, extent, cuts, -0.22, 0.18) * array
    return jnp.clip(array, min=-limit, max=limit).astype(kind)


def setup_inputs(seed: int = 0, part: int = 0) -> dict:
    splits = jax.random.split(jax.random.key(seed), 10)
    part_keys = jax.random.split(jax.random.fold_in(splits[9], part), 10)
    return {
        "residual_pool": draw_residual_pool(jax.random.fold_in(jax.random.fold_in(splits[9], part), 71), part),
        "inner_pool": normal_values(part_keys[1], (SLIDES, POOL, HW, HW, C), 1.0, 6.0, ((0, 4), (1, 4))),
        "window_index": draw_window_index(jax.random.fold_in(jax.random.fold_in(splits[9], part), 71), part),
        "labels": set_ends(jax.random.randint(part_keys[3], (SLIDES,), 0, NCLS), jax.random.fold_in(part_keys[3], 1), 0, NCLS - 1).astype(jnp.int32),
        "group_weight": draw_group_weight(jax.random.fold_in(splits[9], 71), part),
        "expand_weight": normal_values(splits[5], (C, C), C ** -0.5, 0.125),
        "attn_proj": normal_values(splits[6], (2, C, ATT), (C // 16) ** -0.5, 0.5),
        "attn_vector": jnp.clip(jax.random.uniform(splits[7], (ATT, HEADS), jnp.float32, -0.29882812, 0.29882812), -0.29882812, 0.29882812).astype(jnp.bfloat16),
        "classifier": normal_values(splits[8], (HEADS, C, NCLS), (HEADS * C) ** -0.5, 0.046875),
    }


exact_mode = lax.Precision.HIGHEST

def grouped_conv(activated, kernel):
    return lax.conv_general_dilated(activated.astype(jnp.float32), kernel.astype(jnp.float32), (1, 1), 'SAME', dimension_numbers=('NHWC', 'HWIO', 'NHWC'), feature_group_count=GROUPS, precision=exact_mode)

def direction_of(gradient):
    return gradient / (jnp.sqrt(jnp.mean(gradient * gradient)) + 1e-06)

def reference(residual_pool, inner_pool, window_index, labels, group_weight, expand_weight, attn_proj, attn_vector, classifier):
    class_f = classifier.astype(jnp.float32)
    vector_f = attn_vector.astype(jnp.float32)
    proj_f = attn_proj.astype(jnp.float32)
    block_base = jnp.arange(WINDOW, dtype=jnp.int32) // TILE_DEV * POOL_DEV

    def one_slide(running, slide_data):
        res_maps, inner_maps, slide_index, slide_label = slide_data
        pool_rows = (block_base + slide_index.astype(jnp.int32)).astype(jnp.int32)
        picked_res = jnp.take(res_maps, pool_rows, axis=0)
        picked_inner = jnp.take(inner_maps, pool_rows, axis=0)
        activated = jnp.maximum(picked_inner, 0)
        grouped = grouped_conv(activated, group_weight)
        grouped_rows = grouped.reshape(WINDOW * HW * HW, C)
        mid_rows = jnp.maximum(grouped_rows, 0.0).astype(jnp.bfloat16)
        pre_act = jnp.dot(mid_rows, expand_weight, preferred_element_type=jnp.float32) + picked_res.reshape(WINDOW * HW * HW, C).astype(jnp.float32)
        pre_cells = pre_act.reshape(WINDOW, HW * HW, C)
        features = lax.optimization_barrier(jnp.mean(jnp.maximum(pre_cells, 0.0), axis=1)).astype(jnp.bfloat16)
        features_f = features.astype(jnp.float32)
        projected = jnp.einsum('wc,kca->kwa', features_f, proj_f, precision=exact_mode)
        tan_part = jnp.tanh(projected[0])
        sig_part = jax.nn.sigmoid(projected[1])
        gated = (tan_part * sig_part).astype(jnp.bfloat16)
        scores = jnp.dot(gated, attn_vector, preferred_element_type=jnp.float32)
        weights = jnp.exp(scores)
        weight_sum = lax.optimization_barrier(jnp.sum(weights, axis=0))
        pooled = jnp.einsum('wh,wc->hc', weights, features_f, precision=exact_mode) / weight_sum[:, None]
        logits = jnp.einsum('hc,hck->k', pooled, class_f, precision=exact_mode)
        exp_logits = jnp.exp(logits)
        exp_total = jnp.sum(exp_logits)
        onehot = (jnp.arange(NCLS, dtype=jnp.int32) == slide_label).astype(jnp.float32)
        slide_loss = jnp.log(exp_total) - jnp.sum(onehot * logits)
        dlogits = exp_logits / exp_total - onehot
        class_grad = pooled[:, :, None] * dlogits[None, None, :]
        dpooled = jnp.einsum('k,hck->hc', dlogits, class_f, precision=exact_mode)
        attn_share = weights / weight_sum[None, :]
        tile_dots = jnp.einsum('hc,wc->wh', dpooled, features_f, precision=exact_mode)
        pool_dots = lax.optimization_barrier(jnp.sum(dpooled * pooled, axis=1))
        dscores = attn_share * (tile_dots - pool_dots[None, :])
        vector_grad = jnp.einsum('wa,wh->ah', gated.astype(jnp.float32), dscores, precision=exact_mode)
        dgated = jnp.einsum('wh,ah->wa', dscores, vector_f, precision=exact_mode)
        dgate = jnp.stack([dgated * (1.0 - tan_part * tan_part) * sig_part, dgated * tan_part * sig_part * (1.0 - sig_part)]).astype(jnp.bfloat16)
        dgate_f = dgate.astype(jnp.float32)
        proj_grad = jnp.einsum('wc,kwa->kca', features_f, dgate_f, precision=exact_mode)
        dfeatures = jnp.einsum('wh,hc->wc', attn_share, dpooled, precision=exact_mode) + jnp.einsum('kwa,kca->wc', dgate_f, proj_f, precision=exact_mode)
        dpre_rows = jnp.where(pre_cells > 0, dfeatures[:, None, :] / (HW * HW), 0.0).astype(jnp.bfloat16).reshape(WINDOW * HW * HW, C)
        w3_grad = lax.dot_general(mid_rows, dpre_rows, (((0,), (0,)), ((), ())), preferred_element_type=jnp.float32)
        dmid = lax.dot_general(dpre_rows, expand_weight, (((1,), (1,)), ((), ())), preferred_element_type=jnp.float32)
        dgrouped = jnp.where(grouped_rows > 0, dmid, 0.0).astype(jnp.bfloat16)
        unused_out, pullback = jax.vjp(lambda kernel: grouped_conv(activated, kernel), group_weight.astype(jnp.float32))
        w2_grad = pullback(dgrouped.reshape(grouped.shape).astype(jnp.float32))[0]
        updated = (running[0] + w2_grad, running[1] + w3_grad, running[2] + proj_grad, running[3] + vector_grad, running[4] + class_grad)
        return (updated, slide_loss)
    zeros_init = (jnp.zeros(group_weight.shape, jnp.float32), jnp.zeros((C, C), jnp.float32), jnp.zeros(attn_proj.shape, jnp.float32), jnp.zeros(attn_vector.shape, jnp.float32), jnp.zeros(classifier.shape, jnp.float32))
    grad_sums, slide_loss = lax.scan(one_slide, zeros_init, (residual_pool, inner_pool, window_index, labels))
    return (slide_loss, direction_of(grad_sums[0]).astype(jnp.bfloat16), direction_of(grad_sums[1]), direction_of(grad_sums[2]).astype(jnp.bfloat16), direction_of(grad_sums[3]), direction_of(grad_sums[4]))
```

```python
import jax
import jax.numpy as jnp
from jax import lax
from jax.experimental import pallas as pl
from jax.experimental.pallas import tpu as pltpu
from jax.sharding import PartitionSpec as P

C = 2048


exact_mode = lax.Precision.HIGHEST
eps_small = 1e-06


BLOCK = 256
LIMIT = 40 * 1024 * 1024


def pick_rows(pool_maps, local_index, relu):
    stored = jnp.transpose(pool_maps, (1, 2, 3, 0, 4))
    spots = jnp.transpose(local_index)[None, None, :, :, None]
    picked = jnp.broadcast_to(
        stored[0][:, :, None], stored.shape[1:3] + (local_index.shape[1],) + stored.shape[3:]
    )
    for place in range(1, stored.shape[0]):
        picked = jnp.where(spots == place, stored[place][:, :, None], picked)
    if relu:
        picked = jnp.maximum(picked, 0)
    picked = jnp.pad(picked, ((0, 0), (0, 1), (0, 0), (0, 0), (0, 0)))
    return picked.reshape(-1, picked.shape[-1])


def fill_padded(x_ref, padded, edge):
    rows = x_ref.shape[0]
    zeros = jnp.zeros((edge, padded.shape[1]), padded.dtype)
    padded[0:edge, :] = zeros
    padded[edge + rows : edge + rows + edge, :] = zeros
    padded[edge : edge + rows, :] = x_ref[...]


def tap_slices(padded, rows, edge, line, cell):
    taps = []
    for tap_y in range(3):
        for tap_x in range(3):
            start = edge + (tap_y - 1) * line + (tap_x - 1) * cell
            taps.append(padded[start : start + rows, :])
    return taps


def conv_kernel(edge, line, cell, x_ref, w_ref, mid_ref, padded, dense):
    rows, width = x_ref.shape
    group = w_ref.shape[2]
    fill_padded(x_ref, padded, edge)
    own = lax.broadcasted_iota(jnp.int32, (width, width), 0) // group
    other = lax.broadcasted_iota(jnp.int32, (width, width), 1) // group
    same = (own == other).astype(jnp.float32).astype(jnp.bfloat16)
    for tap in range(9):
        small = w_ref[tap // 3, tap % 3]
        dense[tap * width : (tap + 1) * width, :] = (
            jnp.concatenate([small] * (width // group), axis=0) * same
        )
    lhs = jnp.concatenate(tap_slices(padded, rows, edge, line, cell), axis=1)
    grouped = jnp.dot(lhs, dense[...], preferred_element_type=jnp.float32)
    place = lax.broadcasted_iota(jnp.int32, (rows, width), 0) % line
    mid_ref[...] = jnp.where(place < line - cell, jnp.maximum(grouped, 0.0), 0.0).astype(
        jnp.bfloat16
    )


def grouped_forward(x_rows, group_weight, line, cell):
    rows, chans = x_rows.shape
    group = group_weight.shape[2]
    edge = line + 2 * cell
    return pl.pallas_call(
        lambda *refs: conv_kernel(edge, line, cell, *refs),
        grid=(chans // BLOCK,),
        in_specs=[
            pl.BlockSpec((rows, BLOCK), lambda i: (0, i)),
            pl.BlockSpec((3, 3, group, BLOCK), lambda i: (0, 0, 0, i)),
        ],
        out_specs=pl.BlockSpec((rows, BLOCK), lambda i: (0, i)),
        out_shape=jax.ShapeDtypeStruct((rows, chans), jnp.bfloat16),
        scratch_shapes=[
            pltpu.VMEM((rows + 2 * edge, BLOCK), jnp.bfloat16),
            pltpu.VMEM((9 * BLOCK, BLOCK), jnp.bfloat16),
        ],
        compiler_params=pltpu.CompilerParams(vmem_limit_bytes=LIMIT),
        name="grouped_forward",
    )(x_rows, group_weight)


def weight_kernel(edge, line, cell, x_ref, d_ref, out_ref, padded):
    rows, width = x_ref.shape
    group = out_ref.shape[2]
    fill_padded(x_ref, padded, edge)
    turned = jnp.transpose(d_ref[...])
    for tap, shifted in enumerate(tap_slices(padded, rows, edge, line, cell)):
        full = jnp.dot(turned, shifted, preferred_element_type=jnp.float32)
        own = jnp.concatenate(
            [
                full[at : at + group, at : at + group]
                for at in range(0, width, group)
            ],
            axis=0,
        )
        out_ref[tap // 3, tap % 3] = jnp.transpose(own).astype(out_ref.dtype)


def grouped_weight_grad(x_rows, d_rows, group, line, cell):
    rows, chans = x_rows.shape
    edge = line + 2 * cell
    return pl.pallas_call(
        lambda *refs: weight_kernel(edge, line, cell, *refs),
        grid=(chans // BLOCK,),
        in_specs=[
            pl.BlockSpec((rows, BLOCK), lambda i: (0, i)),
            pl.BlockSpec((rows, BLOCK), lambda i: (0, i)),
        ],
        out_specs=pl.BlockSpec((3, 3, group, BLOCK), lambda i: (0, 0, 0, i)),
        out_shape=jax.ShapeDtypeStruct((3, 3, group, chans), jnp.bfloat16),
        scratch_shapes=[pltpu.VMEM((rows + 2 * edge, BLOCK), jnp.bfloat16)],
        compiler_params=pltpu.CompilerParams(vmem_limit_bytes=LIMIT),
        name="grouped_weight_grad",
    )(x_rows, d_rows)


def direction_of(gradient, square_sum, entries):
    return gradient / (jnp.sqrt(square_sum / entries) + eps_small)


def local(
    residual_pool,
    inner_pool,
    window_index,
    labels,
    group_weight,
    expand_weight,
    attn_proj,
    attn_vector,
    classifier,
):
    slides_here = inner_pool.shape[0]
    map_side = inner_pool.shape[2]
    half_chan = inner_pool.shape[4]
    tiles_here = window_index.shape[1]
    group_width = group_weight.shape[2]
    head_count = attn_vector.shape[1]
    class_count = classifier.shape[2]
    att_width = attn_proj.shape[2]
    cell_count = map_side * map_side
    tile_total = slides_here * tiles_here
    line = (map_side + 1) * tile_total
    residual_rows = pick_rows(residual_pool, window_index, False)
    x_rows = pick_rows(inner_pool, window_index, True)
    mid_rows = grouped_forward(x_rows, group_weight, line, tile_total)
    mid_full = lax.all_gather(mid_rows, "chan", axis=1, tiled=True)
    pre_act = jnp.dot(mid_full, expand_weight, preferred_element_type=jnp.float32) + residual_rows
    pre_cells = pre_act.reshape(-1, tile_total, half_chan)
    features = (jnp.sum(jnp.maximum(pre_cells, 0.0), axis=0) / cell_count).astype(jnp.bfloat16)
    slide_devs = lax.axis_size("slide")
    tile_devs = lax.axis_size("tile")
    onehot_here = (
        labels[:, None] == jnp.arange(half_chan, dtype=jnp.int32)[None, :]
    ).astype(jnp.bfloat16)
    packet = jnp.concatenate([features, onehot_here], axis=0)
    gathered = lax.all_gather(packet, ("tile", "slide"), axis=0, tiled=False)
    slides_all = slide_devs * slides_here
    rows_all = tile_devs * slide_devs * tile_total
    feats = gathered[:, :tile_total].reshape(rows_all, half_chan)
    onehot = (
        gathered[:slide_devs, tile_total:, :class_count]
        .astype(jnp.float32)
        .reshape(slides_all, class_count)
    )
    row_at = jnp.arange(rows_all, dtype=jnp.int32)
    row_slide = (row_at // tile_total) % slide_devs * slides_here + row_at % slides_here
    select = (row_slide[:, None] == jnp.arange(slides_all, dtype=jnp.int32)[None, :]).astype(
        jnp.float32
    )
    feats_f = feats.astype(jnp.float32)
    class_f = jnp.transpose(classifier.astype(jnp.float32), (2, 0, 1))
    vector_f = attn_vector.astype(jnp.float32)
    proj_part = jnp.einsum("pc,kca->kpa", feats, attn_proj, preferred_element_type=jnp.float32)
    projected = lax.psum(proj_part, "chan")
    tan_part = jnp.tanh(projected[0])
    sig_part = jax.nn.sigmoid(projected[1])
    gated = (tan_part * sig_part).astype(jnp.bfloat16)
    scores = jnp.dot(gated, attn_vector, preferred_element_type=jnp.float32)
    weights = jnp.exp(scores)
    weight_sum = jnp.einsum("ps,ph->sh", select, weights, precision=exact_mode)
    spread = (select[:, :, None] * weights[:, None, :]).reshape(rows_all, slides_all * head_count)
    pooled_sum = jnp.einsum("pq,pc->qc", spread, feats_f, precision=exact_mode)
    pooled = pooled_sum.reshape(slides_all, head_count, half_chan) / weight_sum[:, :, None]
    logits = lax.psum(jnp.sum(pooled[:, None] * class_f[None], axis=(2, 3)), "chan")
    exp_logits = jnp.exp(logits)
    exp_total = jnp.sum(exp_logits, axis=1)
    loss_all = jnp.log(exp_total) - jnp.sum(onehot * logits, axis=1)
    dlogits = exp_logits / exp_total[:, None] - onehot
    dpooled = jnp.sum(dlogits[:, :, None, None] * class_f[None], axis=1)
    dots = jnp.einsum(
        "qc,pc->pq",
        dpooled.reshape(slides_all * head_count, half_chan),
        feats_f,
        precision=exact_mode,
    ).reshape(rows_all, slides_all, head_count)
    tile_dots, pool_dots = lax.psum(
        (jnp.sum(dots * select[:, :, None], axis=1), jnp.sum(dpooled * pooled, axis=2)), "chan"
    )
    row_sum = jnp.einsum("ps,sh->ph", select, weight_sum, precision=exact_mode)
    row_dots = jnp.einsum("ps,sh->ph", select, pool_dots, precision=exact_mode)
    attn_share = weights / row_sum
    dscores = attn_share * (tile_dots - row_dots)
    grad_vector = jnp.einsum("pa,ph->ah", gated.astype(jnp.float32), dscores, precision=exact_mode)
    dgated = jnp.einsum("ph,ah->pa", dscores, vector_f, precision=exact_mode)
    dgate = jnp.stack(
        [
            dgated * (1.0 - tan_part * tan_part) * sig_part,
            dgated * tan_part * sig_part * (1.0 - sig_part),
        ],
        axis=0,
    ).astype(jnp.bfloat16)
    grad_proj = jnp.einsum("pc,kpa->kca", feats, dgate, preferred_element_type=jnp.float32)
    grad_class = jnp.transpose(
        jnp.sum(dlogits[:, :, None, None] * pooled[:, None], axis=0), (1, 2, 0)
    )
    slide_at = lax.axis_index("slide")
    device_at = lax.axis_index("tile") * slide_devs + slide_at
    slide_loss = lax.dynamic_slice_in_dim(loss_all, slide_at * slides_here, slides_here)
    share_here = lax.dynamic_slice_in_dim(attn_share, device_at * tile_total, tile_total).reshape(
        tiles_here, slides_here, head_count
    )
    dpool_here = lax.dynamic_slice_in_dim(dpooled, slide_at * slides_here, slides_here)
    dgate_here = lax.dynamic_slice_in_dim(dgate, device_at * tile_total, tile_total, axis=1)
    dfeatures = jnp.einsum("tsh,shc->tsc", share_here, dpool_here, precision=exact_mode).reshape(
        tile_total, half_chan
    ) + jnp.einsum("kta,kca->tc", dgate_here, attn_proj, preferred_element_type=jnp.float32)
    dpre_rows = (
        jnp.where(pre_cells > 0, dfeatures[None] / cell_count, 0.0)
        .astype(jnp.bfloat16)
        .reshape(-1, half_chan)
    )
    w3_part = lax.dot_general(
        mid_full, dpre_rows, (((0,), (0,)), ((), ())), preferred_element_type=jnp.float32
    )
    grad_w3 = lax.psum_scatter(
        w3_part.astype(jnp.bfloat16), ("tile", "slide"), scatter_dimension=0, tiled=True
    ).astype(jnp.float32)
    mid_part = lax.dot_general(
        dpre_rows, expand_weight, (((1,), (1,)), ((), ())), preferred_element_type=jnp.float32
    )
    dmid = lax.psum_scatter(
        mid_part.astype(jnp.bfloat16), "chan", scatter_dimension=1, tiled=True
    ).astype(jnp.float32)
    d_rows = jnp.where(mid_rows > 0, dmid, 0.0).astype(jnp.bfloat16)
    w2_part = grouped_weight_grad(x_rows, d_rows, group_width, line, tile_total)
    grad_w2 = lax.psum(w2_part, ("tile", "slide")).astype(jnp.float32)
    w3_square = lax.psum(jnp.sum(grad_w3 * grad_w3), ("tile", "slide", "chan"))
    square_sums = (w3_square,) + lax.psum(
        (
            jnp.sum(grad_w2 * grad_w2),
            jnp.sum(grad_proj * grad_proj),
            jnp.sum(grad_vector * grad_vector) / lax.axis_size("chan"),
            jnp.sum(grad_class * grad_class),
        ),
        "chan",
    )
    dir_w3 = direction_of(grad_w3, square_sums[0], C * C)
    dir_w2 = direction_of(grad_w2, square_sums[1], 9 * group_width * C).astype(jnp.bfloat16)
    dir_proj = direction_of(grad_proj, square_sums[2], 2 * C * att_width).astype(jnp.bfloat16)
    dir_vector = direction_of(grad_vector, square_sums[3], att_width * head_count)
    dir_class = direction_of(grad_class, square_sums[4], head_count * C * class_count)
    return (slide_loss, dir_w2, dir_w3, dir_proj, dir_vector, dir_class)


def solution(mesh):
    return jax.shard_map(
        local,
        mesh=mesh,
        in_specs=(
            P(("parts", "slide"), "tile", None, None, "chan"),
            P(("parts", "slide"), "tile", None, None, "chan"),
            P(("parts", "slide"), "tile"),
            P(("parts", "slide")),
            P(None, None, None, "chan"),
            P(None, "chan"),
            P(None, "chan", None),
            P(),
            P(None, "chan", None),
        ),
        out_specs=(
            P(("parts", "slide")),
            P("parts", None, None, "chan"),
            P(("parts", "tile", "slide"), "chan"),
            P("parts", "chan", None),
            P("parts", None),
            P("parts", "chan", None),
        ),
        check_vma=False,
    )
```

```python
import jax
import jax.numpy as jnp
from jax import lax
from jax.experimental import pallas as pl
from jax.experimental.pallas import tpu as pltpu
from jax.sharding import PartitionSpec as P

C = 2048


exact_mode = lax.Precision.HIGHEST
eps_small = 1e-06


BLOCK = 256
LANES = 128
CHUNKS = 4
LIMIT = 40 * 1024 * 1024


def pick_rows(pool_maps, local_index, relu):
    stored = jnp.transpose(pool_maps, (1, 2, 3, 0, 4))
    spots = jnp.transpose(local_index)[None, None, :, :, None]
    picked = jnp.broadcast_to(
        stored[0][:, :, None], stored.shape[1:3] + (local_index.shape[1],) + stored.shape[3:]
    )
    for place in range(1, stored.shape[0]):
        picked = jnp.where(spots == place, stored[place][:, :, None], picked)
    if relu:
        picked = jnp.maximum(picked, 0)
    picked = lax.optimization_barrier(picked)
    return picked.reshape(-1, picked.shape[-1])


def fill_padded(x_ref, padded, edge, line, cell):
    filled = line - cell
    for at in range(x_ref.shape[0] // filled):
        start = edge + at * line
        padded[start : start + filled, :] = x_ref[at * filled : (at + 1) * filled, :]
        padded[start + filled : start + line, :] = jnp.zeros((cell, padded.shape[1]), padded.dtype)
    if edge:
        zeros = jnp.zeros((edge, padded.shape[1]), padded.dtype)
        padded[0:edge, :] = zeros
        padded[padded.shape[0] - edge :, :] = zeros


def tap_slices(padded, rows, edge, line, cell):
    taps = []
    for tap_y in range(3):
        for tap_x in range(3):
            start = edge + (tap_y - 1) * line + (tap_x - 1) * cell
            taps.append(padded[start : start + rows, :])
    return taps


def conv_kernel(edge, line, cell, x_ref, w_ref, mid_ref, padded, dense):
    width = x_ref.shape[1]
    rows = padded.shape[0] - 2 * edge
    filled = line - cell
    group = w_ref.shape[2]
    fill_padded(x_ref, padded, edge, line, cell)
    own = lax.broadcasted_iota(jnp.int32, (width, width), 0) // group
    other = lax.broadcasted_iota(jnp.int32, (width, width), 1) // group
    same = (own == other).astype(jnp.float32).astype(jnp.bfloat16)
    for tap in range(9):
        small = w_ref[tap // 3, tap % 3]
        dense[tap * width : (tap + 1) * width, :] = (
            jnp.concatenate([small] * (width // group), axis=0) * same
        )
    lhs = jnp.concatenate(tap_slices(padded, rows, edge, line, cell), axis=1)
    grouped = jnp.dot(lhs, dense[...], preferred_element_type=jnp.float32)
    mid = jnp.maximum(grouped, 0.0)
    for at in range(rows // line):
        mid_ref[at * filled : (at + 1) * filled, :] = mid[
            at * line : at * line + filled, :
        ].astype(jnp.bfloat16)


def grouped_forward(x_rows, group_weight, line, cell):
    rows, chans = x_rows.shape
    group = group_weight.shape[2]
    edge = line + 2 * cell
    return pl.pallas_call(
        lambda *refs: conv_kernel(edge, line, cell, *refs),
        grid=(chans // BLOCK,),
        in_specs=[
            pl.BlockSpec((rows, BLOCK), lambda i: (0, i)),
            pl.BlockSpec((3, 3, group, BLOCK), lambda i: (0, 0, 0, i)),
        ],
        out_specs=pl.BlockSpec((rows, BLOCK), lambda i: (0, i)),
        out_shape=jax.ShapeDtypeStruct((rows, chans), jnp.bfloat16),
        scratch_shapes=[
            pltpu.VMEM((rows // (line - cell) * line + 2 * edge, BLOCK), jnp.bfloat16),
            pltpu.VMEM((9 * BLOCK, BLOCK), jnp.bfloat16),
        ],
        compiler_params=pltpu.CompilerParams(vmem_limit_bytes=LIMIT),
        name="grouped_forward",
    )(x_rows, group_weight)


def weight_kernel(edge, line, cell, x_ref, d_ref, out_ref, padded, d_padded):
    width = x_ref.shape[1]
    rows = padded.shape[0] - 2 * edge
    part_width = out_ref.shape[2]
    group = out_ref.shape[1] // 9
    fill_padded(x_ref, padded, edge, line, cell)
    fill_padded(d_ref, d_padded, 0, line, cell)
    turned = jnp.transpose(d_padded[...])
    for tap, shifted in enumerate(tap_slices(padded, rows, edge, line, cell)):
        full = jnp.dot(turned, shifted, preferred_element_type=jnp.float32)
        own = jnp.concatenate(
            [
                full[at : at + group, at : at + group]
                for at in range(0, width, group)
            ],
            axis=0,
        )
        turned_back = jnp.transpose(own).astype(out_ref.dtype)
        for part in range(width // part_width):
            out_ref[part, tap * group : (tap + 1) * group, :] = turned_back[
                :, part * part_width : (part + 1) * part_width
            ]


def grouped_weight_grad(x_rows, d_rows, group, line, cell):
    rows, chans = x_rows.shape
    edge = line + 2 * cell
    return pl.pallas_call(
        lambda *refs: weight_kernel(edge, line, cell, *refs),
        grid=(chans // BLOCK,),
        in_specs=[
            pl.BlockSpec((rows, BLOCK), lambda i: (0, i)),
            pl.BlockSpec((rows, BLOCK), lambda i: (0, i)),
        ],
        out_specs=pl.BlockSpec((BLOCK // LANES, 9 * group, LANES), lambda i: (i, 0, 0)),
        out_shape=jax.ShapeDtypeStruct((chans // LANES, 9 * group, LANES), jnp.bfloat16),
        scratch_shapes=[
            pltpu.VMEM((rows // (line - cell) * line + 2 * edge, BLOCK), jnp.bfloat16),
            pltpu.VMEM((rows // (line - cell) * line, BLOCK), jnp.bfloat16),
        ],
        compiler_params=pltpu.CompilerParams(vmem_limit_bytes=LIMIT),
        name="grouped_weight_grad",
    )(x_rows, d_rows)


def places():
    tile_at, slide_at = lax.axis_index("tile"), lax.axis_index("slide")
    return tile_at, slide_at // 2, slide_at % 2


def remote(src, dst, sems, item, step, tile_to, x_to, core_to):
    send, recv = sems
    return pltpu.make_async_remote_copy(
        src_ref=src,
        dst_ref=dst,
        send_sem=send.at[item, step],
        recv_sem=recv.at[item, step],
        device_id={"tile": tile_to, "slide": x_to * 2 + core_to},
        device_id_type=pl.DeviceIdType.MESH,
    )


def entry_barrier():
    z, x, c = places()
    barrier = pltpu.get_barrier_semaphore()
    peers = [(z, x, 1 - c), (z, 1 - x, c)] + [((z + d) % 4, x, c) for d in (1, 2, 3)]
    for tile_to, x_to, core_to in peers:
        pl.semaphore_signal(
            barrier,
            inc=1,
            device_id={"tile": tile_to, "slide": x_to * 2 + core_to},
            device_id_type=pl.DeviceIdType.MESH,
        )
    pl.semaphore_wait(barrier, len(peers))


def gather_tile(gat, sems, item):
    z, x, c = places()
    own = gat.at[z, x, c]
    return [remote(own, own, sems, item, d - 1, (z + d) % 4, x, c) for d in (1, 2, 3)]


def gather_x(gat, sems, item):
    z, x, c = places()
    own = gat.at[:, x, c]
    return [remote(own, own, sems, item, 3, z, 1 - x, c)]


def gather_core(gat, sems, item):
    z, x, c = places()
    own = gat.at[:, :, c]
    return [remote(own, own, sems, item, 4, z, x, 1 - c)]


def start_all(copies):
    for copy in copies:
        copy.start()
    return copies


def wait_all(copies):
    for copy in copies:
        copy.wait()


def gather_kernel(own_ref, gat, send, recv):
    z, x, c = places()
    sems = (send, recv)
    entry_barrier()
    gat[z, x, c] = own_ref[...]
    wait_all(start_all(gather_tile(gat, sems, 0)))
    wait_all(start_all(gather_x(gat, sems, 0)))
    wait_all(start_all(gather_core(gat, sems, 0)))


def gather_packets(packet):
    return pl.pallas_call(
        gather_kernel,
        in_specs=[pl.BlockSpec(memory_space=pltpu.VMEM)],
        out_specs=pl.BlockSpec(memory_space=pltpu.VMEM),
        out_shape=jax.ShapeDtypeStruct((4, 2, 2) + packet.shape, packet.dtype),
        scratch_shapes=[pltpu.SemaphoreType.DMA((1, 5)), pltpu.SemaphoreType.DMA((1, 5))],
        compiler_params=pltpu.CompilerParams(
            collective_id=1, has_side_effects=True, vmem_limit_bytes=LIMIT
        ),
        name="gather_packets",
    )(packet)


def reduce_kernel(
    entries3,
    entries2,
    w3_ref,
    w2_ref,
    dir3_ref,
    dir2_ref,
    core3,
    side3,
    line3,
    core2,
    side2,
    line2,
    gat,
    squares,
    send,
    recv,
):
    z, x, c = places()
    sems = (send, recv)
    wide = w3_ref.shape[4] // CHUNKS
    f32 = jnp.float32

    def parts(item):
        if item == 0:
            return w2_ref.at, core2, side2, line2, slice(None)
        at = item - 1
        return w3_ref.at, core3.at[at], side3.at[at], line3.at[at], slice(at * wide, (at + 1) * wide)

    def first(item):
        whole, got, _, _, cols = parts(item)
        return [remote(whole[:, :, 1 - c, :, cols], got, sems, item, 0, z, x, 1 - c)]

    def second(item):
        _, got, other, _, _ = parts(item)
        return [remote(got.at[:, 1 - x], other, sems, item, 1, z, 1 - x, c)]

    def third(item):
        _, _, other, ends, _ = parts(item)
        return [
            remote(other.at[(z + d) % 4], ends.at[d - 1], sems, item, 1 + d, (z + d) % 4, x, c)
            for d in (1, 2, 3)
        ]

    def after_first(item):
        _, got, _, _, cols = parts(item)
        wait_all(copies1[item])
        source = w2_ref if item == 0 else w3_ref

        def add(at, carry):
            row, col = at // 2, at % 2
            got[row, col] = (
                source[row, col, c, :, cols].astype(f32) + got[row, col].astype(f32)
            ).astype(jnp.bfloat16)
            return carry

        lax.fori_loop(0, 8, add, 0)
        copies2[item] = start_all(second(item))

    def after_second(item):
        _, got, other, _, _ = parts(item)
        wait_all(copies2[item])

        def add(row, carry):
            other[row] = (got[row, x].astype(f32) + other[row].astype(f32)).astype(jnp.bfloat16)
            return carry

        lax.fori_loop(0, 4, add, 0)
        copies3[item] = start_all(third(item))

    def total(item):
        _, _, other, ends, _ = parts(item)
        wait_all(copies3[item])
        return ((other[z].astype(f32) + ends[0].astype(f32)) + ends[1].astype(f32)) + ends[
            2
        ].astype(f32)

    def fold(values):
        flat = values.reshape(values.shape[0] // 8, 8, values.shape[1])
        flat = jnp.sum(flat * flat, axis=0)
        out = flat[:, 0:LANES]
        for at in range(LANES, flat.shape[1], LANES):
            out = out + flat[:, at : at + LANES]
        return out

    def finish(item):
        value = total(item)
        dir3_ref[:, (item - 1) * wide : item * wide] = value
        return fold(value)

    def scale(tile_sum, entries):
        return 1.0 / (jnp.sqrt(jnp.sum(tile_sum, keepdims=True) / entries) + eps_small)

    copies1, copies2, copies3 = {}, {}, {}
    last = CHUNKS
    entry_barrier()
    for item in range(last + 1):
        copies1[item] = start_all(first(item))
    after_first(0)
    after_first(1)
    after_second(0)
    after_first(2)
    after_second(1)
    gat[z, x, c] = total(0).astype(jnp.bfloat16)
    gathering = start_all(gather_tile(gat, sems, last + 1))
    after_first(3)
    after_second(2)
    square = finish(1)
    wait_all(gathering)
    gathering = start_all(gather_x(gat, sems, last + 1))
    after_first(4)
    after_second(3)
    square = square + finish(2)
    wait_all(gathering)
    gathering = start_all(gather_core(gat, sems, last + 1))
    after_second(4)
    square = square + finish(3)
    wait_all(gathering)

    def square2(at, carry):
        return carry + fold(gat[at // 4, at // 2 % 2, at % 2].astype(f32))

    scale2 = scale(lax.fori_loop(0, 16, square2, jnp.zeros((8, LANES), f32)), entries2)
    for at in range(16):
        dir2_ref[:, at * LANES : (at + 1) * LANES] = (
            gat[at // 4, at // 2 % 2, at % 2].astype(f32) * scale2
        ).astype(jnp.bfloat16)
    square = square + finish(4)
    squares[0] = square
    item = last + 2
    wait_all(start_all([remote(squares.at[0], squares.at[1], sems, item, 0, z, x, 1 - c)]))
    squares[2] = squares[0] + squares[1]
    wait_all(start_all([remote(squares.at[2], squares.at[3], sems, item, 1, z, 1 - x, c)]))
    squares[4] = squares[2] + squares[3]
    wait_all(
        start_all(
            [
                remote(squares.at[4], squares.at[4 + d], sems, item, 1 + d, (z + d) % 4, x, c)
                for d in (1, 2, 3)
            ]
        )
    )
    scale3 = scale((squares[4] + squares[5]) + (squares[6] + squares[7]), entries3)
    dir3_ref[...] = dir3_ref[...] * scale3


def reduce_directions(w3_part, w2_part, entries3, entries2):
    depth, chans = w3_part.shape
    rows3 = depth // 16
    rows2 = w2_part.shape[1]
    wide = chans // CHUNKS
    half = jnp.bfloat16
    vmem = pl.BlockSpec(memory_space=pltpu.VMEM)
    return pl.pallas_call(
        lambda *refs: reduce_kernel(entries3, entries2, *refs),
        in_specs=[vmem, vmem],
        out_specs=[vmem, vmem],
        out_shape=[
            jax.ShapeDtypeStruct((rows3, chans), jnp.float32),
            jax.ShapeDtypeStruct((rows2, chans), half),
        ],
        scratch_shapes=[
            pltpu.VMEM((CHUNKS, 4, 2, rows3, wide), half),
            pltpu.VMEM((CHUNKS, 4, rows3, wide), half),
            pltpu.VMEM((CHUNKS, 3, rows3, wide), half),
            pltpu.VMEM((4, 2, rows2, LANES), half),
            pltpu.VMEM((4, rows2, LANES), half),
            pltpu.VMEM((3, rows2, LANES), half),
            pltpu.VMEM((4, 2, 2, rows2, LANES), half),
            pltpu.VMEM((8, 8, LANES), jnp.float32),
            pltpu.SemaphoreType.DMA((CHUNKS + 3, 5)),
            pltpu.SemaphoreType.DMA((CHUNKS + 3, 5)),
        ],
        compiler_params=pltpu.CompilerParams(
            collective_id=2, has_side_effects=True, vmem_limit_bytes=LIMIT
        ),
        name="reduce_directions",
    )(w3_part.reshape(4, 2, 2, rows3, chans), w2_part.reshape(4, 2, 2, rows2, LANES))


def direction_of(gradient, square_sum, entries):
    return gradient / (jnp.sqrt(square_sum / entries) + eps_small)


def local(
    residual_pool,
    inner_pool,
    window_index,
    labels,
    group_weight,
    expand_weight,
    attn_proj,
    attn_vector,
    classifier,
):
    slides_here = inner_pool.shape[0]
    map_side = inner_pool.shape[2]
    half_chan = inner_pool.shape[4]
    tiles_here = window_index.shape[1]
    group_width = group_weight.shape[2]
    head_count = attn_vector.shape[1]
    class_count = classifier.shape[2]
    att_width = attn_proj.shape[2]
    cell_count = map_side * map_side
    tile_total = slides_here * tiles_here
    line = (map_side + 1) * tile_total
    residual_rows = pick_rows(residual_pool, window_index, False)
    x_rows = pick_rows(inner_pool, window_index, True)
    mid_rows = grouped_forward(x_rows, group_weight, line, tile_total)
    mid_full = lax.all_gather(mid_rows, "chan", axis=1, tiled=True)
    pre_act = jnp.dot(mid_full, expand_weight, preferred_element_type=jnp.float32) + residual_rows
    pre_cells = pre_act.reshape(-1, tile_total, half_chan)
    features = (jnp.sum(jnp.maximum(pre_cells, 0.0), axis=0) / cell_count).astype(jnp.bfloat16)
    slide_devs = lax.axis_size("slide")
    tile_devs = lax.axis_size("tile")
    onehot_here = (
        labels[:, None] == jnp.arange(half_chan, dtype=jnp.int32)[None, :]
    ).astype(jnp.bfloat16)
    packet = jnp.concatenate([features, onehot_here], axis=0)
    own_kernels = (
        slide_devs == 4 and tile_devs == 4 and lax.axis_size("chan") == 1 and half_chan == 16 * LANES
    )
    if own_kernels:
        spare = -packet.shape[0] % 16
        gathered = gather_packets(jnp.pad(packet, ((0, spare), (0, 0))))
        gathered = gathered.reshape((-1,) + gathered.shape[3:])[:, : packet.shape[0]]
    else:
        gathered = lax.all_gather(packet, ("tile", "slide"), axis=0, tiled=False)
    slides_all = slide_devs * slides_here
    rows_all = tile_devs * slide_devs * tile_total
    feats = gathered[:, :tile_total].reshape(rows_all, half_chan)
    onehot = (
        gathered[:slide_devs, tile_total:, :class_count]
        .astype(jnp.float32)
        .reshape(slides_all, class_count)
    )
    row_at = jnp.arange(rows_all, dtype=jnp.int32)
    row_slide = (row_at // tile_total) % slide_devs * slides_here + row_at % slides_here
    select = (row_slide[:, None] == jnp.arange(slides_all, dtype=jnp.int32)[None, :]).astype(
        jnp.float32
    )
    feats_f = feats.astype(jnp.float32)
    class_f = jnp.transpose(classifier.astype(jnp.float32), (2, 0, 1))
    vector_f = attn_vector.astype(jnp.float32)
    proj_part = jnp.einsum("pc,kca->kpa", feats, attn_proj, preferred_element_type=jnp.float32)
    projected = lax.psum(proj_part, "chan")
    tan_part = jnp.tanh(projected[0])
    sig_part = jax.nn.sigmoid(projected[1])
    gated = (tan_part * sig_part).astype(jnp.bfloat16)
    scores = jnp.dot(gated, attn_vector, preferred_element_type=jnp.float32)
    weights = jnp.exp(scores)
    weight_sum = jnp.einsum("ps,ph->sh", select, weights, precision=exact_mode)
    spread = (select[:, :, None] * weights[:, None, :]).reshape(rows_all, slides_all * head_count)
    pooled_sum = jnp.einsum("pq,pc->qc", spread, feats_f, precision=exact_mode)
    pooled = pooled_sum.reshape(slides_all, head_count, half_chan) / weight_sum[:, :, None]
    logits = lax.psum(jnp.sum(pooled[:, None] * class_f[None], axis=(2, 3)), "chan")
    exp_logits = jnp.exp(logits)
    exp_total = jnp.sum(exp_logits, axis=1)
    loss_all = jnp.log(exp_total) - jnp.sum(onehot * logits, axis=1)
    dlogits = exp_logits / exp_total[:, None] - onehot
    dpooled = jnp.sum(dlogits[:, :, None, None] * class_f[None], axis=1)
    dots = jnp.einsum(
        "qc,pc->pq",
        dpooled.reshape(slides_all * head_count, half_chan),
        feats_f,
        precision=exact_mode,
    ).reshape(rows_all, slides_all, head_count)
    tile_dots, pool_dots = lax.psum(
        (jnp.sum(dots * select[:, :, None], axis=1), jnp.sum(dpooled * pooled, axis=2)), "chan"
    )
    row_sum = jnp.einsum("ps,sh->ph", select, weight_sum, precision=exact_mode)
    row_dots = jnp.einsum("ps,sh->ph", select, pool_dots, precision=exact_mode)
    attn_share = weights / row_sum
    dscores = attn_share * (tile_dots - row_dots)
    grad_vector = jnp.einsum("pa,ph->ah", gated.astype(jnp.float32), dscores, precision=exact_mode)
    dgated = jnp.einsum("ph,ah->pa", dscores, vector_f, precision=exact_mode)
    dgate = jnp.stack(
        [
            dgated * (1.0 - tan_part * tan_part) * sig_part,
            dgated * tan_part * sig_part * (1.0 - sig_part),
        ],
        axis=0,
    ).astype(jnp.bfloat16)
    grad_proj = jnp.einsum("pc,kpa->kca", feats, dgate, preferred_element_type=jnp.float32)
    grad_class = jnp.transpose(
        jnp.sum(dlogits[:, :, None, None] * pooled[:, None], axis=0), (1, 2, 0)
    )
    slide_at = lax.axis_index("slide")
    device_at = lax.axis_index("tile") * slide_devs + slide_at
    slide_loss = lax.dynamic_slice_in_dim(loss_all, slide_at * slides_here, slides_here)
    share_here = lax.dynamic_slice_in_dim(attn_share, device_at * tile_total, tile_total).reshape(
        tiles_here, slides_here, head_count
    )
    dpool_here = lax.dynamic_slice_in_dim(dpooled, slide_at * slides_here, slides_here)
    dgate_here = lax.dynamic_slice_in_dim(dgate, device_at * tile_total, tile_total, axis=1)
    dfeatures = jnp.einsum("tsh,shc->tsc", share_here, dpool_here, precision=exact_mode).reshape(
        tile_total, half_chan
    ) + jnp.einsum("kta,kca->tc", dgate_here, attn_proj, preferred_element_type=jnp.float32)
    dpre_rows = (
        jnp.where(pre_cells > 0, dfeatures[None] / cell_count, 0.0)
        .astype(jnp.bfloat16)
        .reshape(-1, half_chan)
    )
    w3_part = lax.dot_general(
        mid_full, dpre_rows, (((0,), (0,)), ((), ())), preferred_element_type=jnp.float32
    )
    mid_part = lax.dot_general(
        dpre_rows, expand_weight, (((1,), (1,)), ((), ())), preferred_element_type=jnp.float32
    )
    dmid = lax.psum_scatter(
        mid_part.astype(jnp.bfloat16), "chan", scatter_dimension=1, tiled=True
    ).astype(jnp.float32)
    d_rows = jnp.where(mid_rows > 0, dmid, 0.0).astype(jnp.bfloat16)
    w2_part = grouped_weight_grad(x_rows, d_rows, group_width, line, tile_total)
    entries2 = 9 * group_width * C
    if own_kernels:
        dir_w3, dir_w2 = reduce_directions(w3_part.astype(jnp.bfloat16), w2_part, C * C, entries2)
        dir_w2 = dir_w2.reshape(3, 3, group_width, half_chan)
    else:
        grad_w3 = lax.psum_scatter(
            w3_part.astype(jnp.bfloat16), ("tile", "slide"), scatter_dimension=0, tiled=True
        ).astype(jnp.float32)
        grad_w2 = lax.psum(w2_part, ("tile", "slide")).astype(jnp.float32)
        w3_square = lax.psum(jnp.sum(grad_w3 * grad_w3), ("tile", "slide", "chan"))
        w2_square = lax.psum(jnp.sum(grad_w2 * grad_w2), "chan")
        dir_w3 = direction_of(grad_w3, w3_square, C * C)
        dir_w2 = direction_of(grad_w2, w2_square, entries2).astype(jnp.bfloat16)
        dir_w2 = jnp.transpose(dir_w2, (1, 0, 2)).reshape(3, 3, group_width, half_chan)
    square_sums = lax.psum(
        (
            jnp.sum(grad_proj * grad_proj),
            jnp.sum(grad_vector * grad_vector) / lax.axis_size("chan"),
            jnp.sum(grad_class * grad_class),
        ),
        "chan",
    )
    dir_proj = direction_of(grad_proj, square_sums[0], 2 * C * att_width).astype(jnp.bfloat16)
    dir_vector = direction_of(grad_vector, square_sums[1], att_width * head_count)
    dir_class = direction_of(grad_class, square_sums[2], head_count * C * class_count)
    return (slide_loss, dir_w2, dir_w3, dir_proj, dir_vector, dir_class)


def solution(mesh):
    return jax.shard_map(
        local,
        mesh=mesh,
        in_specs=(
            P(("parts", "slide"), "tile", None, None, "chan"),
            P(("parts", "slide"), "tile", None, None, "chan"),
            P(("parts", "slide"), "tile"),
            P(("parts", "slide")),
            P(None, None, None, "chan"),
            P(None, "chan"),
            P(None, "chan", None),
            P(),
            P(None, "chan", None),
        ),
        out_specs=(
            P(("parts", "slide")),
            P("parts", None, None, "chan"),
            P(("parts", "tile", "slide"), "chan"),
            P("parts", "chan", None),
            P("parts", None),
            P("parts", "chan", None),
        ),
        check_vma=False,
    )
```
